128 devices in a mesh: dp: 4 (over y), context: 16 (over x, z), tensor: 2 (over core).
Axes of the slice: x: 4, y: 4, z: 4, core: 2. Of those that a mesh axis runs over, the one named last changes fastest.
Arguments:
- tokens: bfloat16 [4, 8192, 2048], P('dp', 'context'), may hold values from -6 to 6
- cotangent: bfloat16 [4, 8192, 2048], P('dp', 'context'), may hold values from -6 to 6
- query_weight: bfloat16 [2048, 2048], P('dp', 'tensor'), may hold values from -0.125 to 0.125
- key_master: float32 [2048, 2048], P('dp', 'tensor'), may hold values from -0.125 to 0.125
- value_weight: bfloat16 [2048, 2048], P('dp', 'tensor'), may hold values from -0.125 to 0.125
- out_weight: bfloat16 [2048, 2048], P('dp', 'tensor'), may hold values from -0.125 to 0.125
- key_moment: float32 [2048, 2048], P('dp', 'tensor'), may hold values from -6 to 6
- key_second: float32 [2048, 2048], P('dp', 'tensor'), may hold values from 0.65536 to 6.5536
Outputs:
- input_grad: bfloat16 [4, 8192, 2048], P('dp', 'context', 'tensor')
- key_master_new: float32 [2048, 2048], P('dp', 'tensor')
- key_moment_new: float32 [2048, 2048], P('dp', 'tensor')
- key_second_new: float32 [2048, 2048], P('dp', 'tensor')
The draws below stay inside these ranges and needn't reach their ends.
All inputs are finite; a program needn't handle non-finite values.
Results may differ from the reference program's by a relative error of at most 0.012.
The reference program's roundings to bfloat16 on the way (of `key_weight`, `memory_b`, `grad_attended` and `grad_memory`) count: a program that leaves them out, or rounds other values in their place, can miss the bound.
Values may be sent and summed in bfloat16 or wider, within the bound.
No kernel may reach another device: no remote copies, remote signals or barrier semaphores. Data moves between devices by JAX's collectives and lax.ppermute only.
A program may use at most 128 MiB of HBM per device.

```python
import math
import jax
import jax.numpy as jnp
from jax import lax

D = 2048
H = 16
HEAD = 128
HD = 2048
SEQ = 8192
BATCH = 4


def raised(array, own_key, source, target, parts, factor):
    def block_of(dim):
        return (jnp.arange(array.shape[dim]) // (array.shape[dim] // parts)).reshape((-1,) + (1,) * (array.ndim - 1 - dim))

    near = jax.random.permutation(own_key, parts)[block_of(target)]
    second = (block_of(target) + parts // 2) % parts
    return jnp.where((block_of(source) == near) | (block_of(source) == second), factor * array, array)


def shard_levels(key, extent, pieces, smallest, largest):
    gain, own = 1.0, jax.random.fold_in(key, 6)
    for dim, parts in pieces:
        draws = jnp.exp(jax.random.uniform(jax.random.fold_in(own, dim), (parts,), jnp.float32, smallest / len(pieces), largest / len(pieces)))
        gain = gain * jnp.repeat(draws, extent[dim] // parts).reshape([-1 if axis == dim else 1 for axis in range(len(extent))])
    return gain


def centred(rng, shape, spread, most, cuts=(), held_as=jnp.bfloat16):
    values = spread * jax.random.normal(rng, shape, jnp.float32)
    if cuts:
        values = values * shard_levels(rng, shape, cuts, -0.22, 0.18)
    return jnp.clip(values, -most, most).astype(held_as)


def noise_with(own_key, extent, spread, most, shards, heavy, held_as=jnp.bfloat16):
    result = spread * jax.random.normal(own_key, extent, jnp.float32)
    if shards:
        result = result * shard_levels(own_key, extent, shards, -0.22, 0.18)
    return jnp.clip(raised(result, jax.random.fold_in(own_key, 3), *heavy), -most, most).astype(held_as)


def setup_inputs(seed: int = 0) -> dict:
    key_list = jax.random.split(jax.random.key(seed), 9)
    return {
        "tokens": noise_with(key_list[0], (BATCH, SEQ, D), 1.0, 6.0, ((0, 4), (1, 16)), (1, 2, 16, 2.0)),
        "cotangent": centred(key_list[1], (BATCH, SEQ, D), 1.0, 6.0, ((0, 4), (1, 16))),
        "query_weight": centred(key_list[2], (D, HD), D ** -0.5, 0.125, ((0, 4), (1, 2))),
        "key_master": centred(key_list[3], (D, HD), D ** -0.5, 0.125, ((0, 4), (1, 2)), jnp.float32),
        "value_weight": centred(key_list[4], (D, HD), D ** -0.5, 0.125, ((0, 4), (1, 2))),
        "out_weight": centred(key_list[5], (D, HD), D ** -0.5, 0.125, ((0, 4), (1, 2))),
        "key_moment": centred(key_list[6], (D, HD), (0.0125 * (BATCH * SEQ) ** 0.5), 6.0, ((0, 4), (1, 2)), jnp.float32),
        "key_second": jnp.clip(jnp.exp(math.log(6.5536) - 2.3025851 * jax.random.uniform(key_list[7], (D, HD), jnp.float32) ** shard_levels(key_list[7], (D, HD), ((0, 4), (1, 2)), -0.2, 0.2)), 0.65536, 6.5536),
    }


norm_eps = 1e-06
beta_one = 0.9
beta_two = 0.999
bias_one = 0.9999734386011124
bias_two = 0.09520785288
adam_eps = 1e-08
learn_rate = 0.001
weight_decay = 0.1

def adam_update(master, moment, second, gradient):
    moment_new = beta_one * moment + (1.0 - beta_one) * gradient
    second_new = beta_two * second + (1.0 - beta_two) * gradient * gradient
    update = moment_new / bias_one / (jnp.sqrt(second_new / bias_two) + adam_eps)
    master_new = master - learn_rate * (update + weight_decay * master)
    return (master_new, moment_new, second_new)

def reference(tokens, cotangent, query_weight, key_master, value_weight, out_weight, key_moment, key_second):
    flat_tokens = tokens.reshape(BATCH * SEQ, D)
    flat_cotangent = cotangent.reshape(BATCH * SEQ, D)
    key_weight = key_master.astype(jnp.bfloat16)

    def project(weight):
        product = jnp.dot(flat_tokens, weight, preferred_element_type=jnp.float32)
        return product.astype(jnp.bfloat16).reshape(BATCH, SEQ, H, HEAD)
    queries = project(query_weight)
    key_rows = project(key_weight)
    value_rows = project(value_weight)
    memory = jnp.einsum('bshd,bshe->bhde', key_rows.astype(jnp.float32), value_rows.astype(jnp.float32))
    memory_b = memory.astype(jnp.bfloat16)
    attended = jnp.einsum('bshd,bhde->bshe', queries.astype(jnp.float32), memory_b.astype(jnp.float32))
    root_mean = jnp.sqrt(lax.optimization_barrier(jnp.mean(attended * attended, axis=-1, keepdims=True)) + norm_eps)
    normed = attended / root_mean
    grad_normed = jnp.dot(flat_cotangent, out_weight, preferred_element_type=jnp.float32).reshape(BATCH, SEQ, H, HEAD)
    inner = lax.optimization_barrier(jnp.mean(grad_normed * normed, axis=-1, keepdims=True))
    grad_attended = ((grad_normed - normed * inner) / root_mean).astype(jnp.bfloat16)
    grad_memory = jnp.einsum('bshd,bshe->bhde', queries.astype(jnp.float32), grad_attended.astype(jnp.float32))
    grad_memory_b = grad_memory.astype(jnp.bfloat16).astype(jnp.float32)
    memory_f = memory_b.astype(jnp.float32)
    grad_queries = jnp.einsum('bshe,bhde->bshd', grad_attended.astype(jnp.float32), memory_f).astype(jnp.bfloat16)
    grad_keys = jnp.einsum('bshe,bhde->bshd', value_rows.astype(jnp.float32), grad_memory_b).astype(jnp.bfloat16)
    grad_values = jnp.einsum('bshd,bhde->bshe', key_rows.astype(jnp.float32), grad_memory_b).astype(jnp.bfloat16)
    grad_queries = grad_queries.reshape(BATCH * SEQ, HD)
    grad_keys = grad_keys.reshape(BATCH * SEQ, HD)
    grad_values = grad_values.reshape(BATCH * SEQ, HD)
    last_dims = (((1,), (1,)), ((), ()))
    input_terms = lax.dot_general(grad_queries, query_weight, last_dims, preferred_element_type=jnp.float32)
    input_terms = input_terms + lax.dot_general(grad_keys, key_weight, last_dims, preferred_element_type=jnp.float32)
    input_terms = input_terms + lax.dot_general(grad_values, value_weight, last_dims, preferred_element_type=jnp.float32)
    input_grad = input_terms.astype(jnp.bfloat16).reshape(BATCH, SEQ, D)
    gradient = lax.dot_general(flat_tokens, grad_keys, (((0,), (0,)), ((), ())), preferred_element_type=jnp.float32)
    gradient = gradient * (1.0 / BATCH)
    master_new, moment_new, second_new = adam_update(key_master, key_moment, key_second, gradient)
    return (input_grad, master_new, moment_new, second_new)
```

```python
import functools

import jax
import jax.numpy as jnp
from jax import lax
from jax.experimental import pallas as pl
from jax.experimental.pallas import tpu as pltpu
from jax.sharding import PartitionSpec as P

HEAD = 128
BF = jnp.bfloat16
F32 = jnp.float32

norm_eps = 1e-06
beta_one = 0.9
beta_two = 0.999
bias_one = 0.9999734386011124
bias_two = 0.09520785288
adam_eps = 1e-08
learn_rate = 0.001
weight_decay = 0.1

VMEM = pl.BlockSpec(memory_space=pltpu.VMEM)
SMEM = pl.BlockSpec(memory_space=pltpu.SMEM)
CORE = ("context", "tensor")


def y_pairs(shift):
    return [(y, (y + shift) % 4) for y in range(4)]


def plane_target(x, z, core, shift, cross):
    if (core == 0) != cross:
        return ((x + shift) % 4) * 4 + z
    return x * 4 + (z + shift) % 4


def plane_pairs(shift, cross=False):
    return [
        ((x * 4 + z) * 2 + core, plane_target(x, z, core, shift, cross) * 2 + core)
        for x in range(4)
        for z in range(4)
        for core in range(2)
    ]


def plane_groups(cross=False):
    groups = []
    for other in range(4):
        for core in range(2):
            if (core == 0) != cross:
                groups.append([(x * 4 + other) * 2 + core for x in range(4)])
            else:
                groups.append([(other * 4 + z) * 2 + core for z in range(4)])
    return groups


def send_y(block, shift):
    return lax.ppermute(block, "dp", y_pairs(shift))


def send_plane(block, shift, cross=False):
    return lax.ppermute(block, CORE, plane_pairs(shift, cross))


def after(value, *others):
    return lax.optimization_barrier((value,) + others)[0]


def run(kernel, out_shape, args, flops, scalars=True, limit=48):
    specs = [SMEM] + [VMEM] * (len(args) - 1) if scalars else [VMEM] * len(args)
    many = isinstance(out_shape, (list, tuple))
    total = sum(a.size * a.dtype.itemsize for a in args)
    total += sum(o.size * o.dtype.itemsize for o in (out_shape if many else [out_shape]))
    return pl.pallas_call(
        kernel,
        out_shape=out_shape,
        in_specs=specs,
        out_specs=[VMEM] * len(out_shape) if many else VMEM,
        compiler_params=pltpu.CompilerParams(vmem_limit_bytes=limit << 20),
        cost_estimate=pl.CostEstimate(flops=flops, bytes_accessed=total, transcendentals=0),
    )(*args)


def shape(dims, dtype):
    return jax.ShapeDtypeStruct(dims, dtype)


def dot(left, right, left_dim, right_dim):
    return lax.dot_general(
        left, right, (((left_dim,), (right_dim,)), ((), ())), preferred_element_type=F32
    )


def at(index, size):
    return pl.ds(pl.multiple_of(index * size, size), size)


def gather_y(own, place):
    block = lax.dynamic_index_in_dim(own, place, 0, keepdims=False)
    return block


def ring_near(block, first):
    from_minus = send_plane(block, 1)
    from_plus = send_plane(block, -1)
    far = send_plane(from_minus, 1) if first else send_plane(from_plus, -1)
    return [block, from_plus, far, from_minus]


def ring_far(block):
    return [block, send_plane(block, -1), send_plane(block, 2), send_plane(block, 1)]


def gather(own, place):
    block = gather_y(own, place)
    y_minus = send_y(block, 1)
    y_plus = send_y(block, -1)
    y_minus, y_plus = lax.optimization_barrier((y_minus, y_plus))
    y_far = send_y(after(block, y_minus, y_plus), 2)
    one = ring_near(y_plus, False)
    three = ring_near(y_minus, True)
    two = ring_far(y_far)
    return one + two + three, y_far


def block_of(own, blocks, dy, dq, quarter):
    if dy == 0:
        return own[lax.rem(quarter + dq, 4)]
    return blocks[(dy - 1) * 4 + dq][...]


def keys_kernel(where, tokens, own, *refs):
    blocks, (keys, values, memory) = refs[:12], refs[12:]
    y, quarter = where[0], where[1]
    for dq in range(4):
        total = None
        for dy in range(4):
            part = tokens[:, at(lax.rem(y + dy, 4), 512)]
            term = dot(part, block_of(own, blocks, dy, dq, quarter), 1, 0)
            total = term if total is None else total + term
        both = total.astype(BF)
        keys[:, dq * 256 : dq * 256 + 256] = both[:, :256]
        values[:, dq * 256 : dq * 256 + 256] = both[:, 256:]
        for head in range(2):
            low = head * HEAD
            memory[lax.rem(quarter + dq, 4) * 2 + head] = dot(
                both[:, low : low + HEAD], both[:, 256 + low : 256 + low + HEAD], 0, 0
            )


def queries_kernel(where, tokens, cotangent, own, *refs):
    blocks, (queries, grad_normed) = refs[:12], refs[12:]
    y, quarter = where[0], where[1]
    for dq in range(4):
        left = right = None
        for dy in range(4):
            cols = at(lax.rem(y + dy, 4), 512)
            block = block_of(own, blocks, dy, dq, quarter)
            one = dot(tokens[:, cols], block[:, :256], 1, 0)
            two = dot(cotangent[:, cols], block[:, 256:], 1, 0)
            left = one if left is None else left + one
            right = two if right is None else right + two
        queries[:, dq * 256 : dq * 256 + 256] = left.astype(BF)
        grad_normed[:, dq * 256 : dq * 256 + 256] = right


def attend_kernel(where, queries, grad_normed, memory, grad_queries, grad_memory):
    quarter = where[1]
    for head in range(8):
        cols = slice(head * HEAD, head * HEAD + HEAD)
        true_head = lax.rem(quarter * 2 + head, 8)
        query, mem, grad = queries[:, cols], memory[true_head], grad_normed[:, cols]
        attended = dot(query, mem, 1, 0)
        square = jnp.mean(attended * attended, axis=-1, keepdims=True)
        root_mean = jnp.sqrt(square + norm_eps)
        normed = attended / root_mean
        inner = jnp.mean(grad * normed, axis=-1, keepdims=True)
        grad_attended = ((grad - normed * inner) / root_mean).astype(BF)
        grad_memory[true_head] = dot(query, grad_attended, 0, 0)
        grad_queries[:, cols] = dot(grad_attended, mem, 1, 1).astype(BF)


def outer_kernel(where, tokens, values, product):
    quarter, core = where[1], where[2]
    for dq in range(4):
        cols = at(lax.rem(quarter + dq, 4), 256)
        for y in range(4):
            block = dot(tokens[:, y * 512 : y * 512 + 512], values[:, dq * 256 : dq * 256 + 256], 0, 0)
            block = block.astype(BF)
            for x in range(4):
                for z in range(4):
                    row = (x * 4 + z) * 32
                    spot = jnp.where(core == 0, x * 4 + z, z * 4 + x)
                    product[spot, y * 32 : y * 32 + 32, cols] = block[row : row + 32]


def query_grad_kernel(where, grad_queries, own, *refs):
    blocks, out = refs[:12], refs[12]
    y, quarter = where[0], where[1]
    for dy in range(4):
        total = None
        for dq in range(4):
            block = block_of(own, blocks, dy, dq, quarter)[:, :256]
            term = dot(grad_queries[:, dq * 256 : dq * 256 + 256], block, 1, 1)
            total = term if total is None else total + term
        true_y = lax.rem(y + dy, 4)
        out[true_y // 2, :, at(lax.rem(true_y, 2), 512)] = total


def input_grad_kernel(where, query_part, keys, values, grad_memory, own, *refs):
    blocks, out, both = refs[:12], refs[12], refs[13]
    y, quarter = where[0], where[1]
    for dq in range(4):
        for head in range(2):
            low = dq * 256 + head * HEAD
            mem = grad_memory[lax.rem(quarter + dq, 4) * 2 + head]
            grad_key = dot(values[:, low : low + HEAD], mem, 1, 1).astype(BF)
            grad_value = dot(keys[:, low : low + HEAD], mem, 1, 0).astype(BF)
            spot = head * HEAD
            both[dq, :, spot : spot + HEAD] = grad_key
            both[dq, :, 256 + spot : 256 + spot + HEAD] = grad_value
    for dy in range(4):
        true_y = lax.rem(y + dy, 4)
        cols = at(lax.rem(true_y, 2), 512)
        total = query_part[true_y // 2, :, cols]
        for dq in range(4):
            total = total + dot(both[dq], block_of(own, blocks, dy, dq, quarter), 1, 1)
        out[true_y // 2, :, cols] = total


def slice_grad_kernel(product, grad_memory, out):
    for head in range(8):
        cols = slice(head * HEAD, head * HEAD + HEAD)
        part = product[:, cols]
        high = part.astype(BF)
        low = (part - high.astype(F32)).astype(BF)
        mem = grad_memory[head]
        out[:, cols] = (dot(high, mem, 1, 1) + dot(low, mem, 1, 1)) * 0.25


def adam_kernel(where, master, moment, second, one, two, three, four, *outs):
    master_new, moment_new, second_new = outs
    core, x, z = where[2], where[3], where[4]
    for dx, blocks in enumerate((one, two, three, four)):
        for dz in range(4):
            first, other = dz, dx
            place_x = lax.rem(x + jnp.where(core == 0, first, other), 4)
            place_z = lax.rem(z + jnp.where(core == 0, other, first), 4)
            rows = at(place_x * 4 + place_z, 32)
            gradient = blocks[dz * 32 : dz * 32 + 32, :].astype(F32)
            held = master[rows, :]
            moved = beta_one * moment[rows, :] + (1.0 - beta_one) * gradient
            squared = beta_two * second[rows, :] + (1.0 - beta_two) * gradient * gradient
            update = moved / bias_one / (jnp.sqrt(squared / bias_two) + adam_eps)
            master_new[rows, :] = held - learn_rate * (update + weight_decay * held)
            moment_new[rows, :] = moved
            second_new[rows, :] = squared


def sum_over_context(partial):
    pieces = lax.all_to_all(partial.reshape(16, 64, HEAD), "context", 0, 0, tiled=True)
    mine = jnp.sum(pieces, axis=0).astype(BF)
    copies = jnp.broadcast_to(mine[None], (16, 64, HEAD))
    return lax.all_to_all(copies, "context", 0, 0, tiled=True).reshape(8, HEAD, HEAD)


def share_plane(block, cross):
    return [
        block,
        send_plane(block, -1, cross),
        send_plane(block, 2, cross),
        send_plane(block, 1, cross),
    ]


def local(
    tokens, cotangent, query_weight, key_master, value_weight, out_weight, key_moment, key_second
):
    tokens = tokens.reshape(512, 2048)
    cotangent = cotangent.reshape(512, 2048)
    y, context, core = (lax.axis_index(name) for name in ("dp", "context", "tensor"))
    x, z = context // 4, lax.rem(context, 4)
    quarter = jnp.where(core == 0, x, z)
    where = jnp.stack([y, quarter, core, x, z]).astype(jnp.int32)

    def quarters(left, right):
        parts = [w.reshape(512, 4, 256).transpose(1, 0, 2) for w in (left, right)]
        return jnp.concatenate(parts, axis=2)

    kv_own = quarters(key_master.astype(BF), value_weight)
    qo_own = quarters(query_weight, out_weight)

    kv_blocks, kv_sent = gather(kv_own, quarter)
    qo_blocks, _ = gather(after(qo_own, kv_sent), quarter)

    keys, values, partial = run(
        keys_kernel,
        [shape((512, 1024), BF), shape((512, 1024), BF), shape((8, HEAD, HEAD), F32)],
        [where, tokens, kv_own] + kv_blocks,
        4_400_000_000,
    )
    memory = sum_over_context(partial)
    queries, grad_normed = run(
        queries_kernel,
        [shape((512, 1024), BF), shape((512, 1024), F32)],
        [where, tokens, cotangent, qo_own] + qo_blocks,
        4_300_000_000,
    )
    grad_queries, partial = run(
        attend_kernel,
        [shape((512, 1024), BF), shape((8, HEAD, HEAD), F32)],
        [where, queries, grad_normed, memory],
        500_000_000,
    )
    grad_memory = sum_over_context(partial)

    product = run(
        outer_kernel, shape((16, 128, 1024), BF), [where, tokens, values], 2_150_000_000
    )
    pieces = lax.all_to_all(
        product.reshape(4, 512, 1024), CORE, 0, 0, tiled=True, axis_index_groups=plane_groups()
    )
    half = jnp.sum(pieces.astype(F32), axis=0).astype(BF)
    pieces = lax.all_to_all(
        half.reshape(4, 128, 1024), CORE, 0, 0, tiled=True, axis_index_groups=plane_groups(True)
    )
    product = jnp.sum(pieces.astype(F32), axis=0)

    query_part = run(
        query_grad_kernel,
        shape((2, 512, 1024), F32),
        [where, grad_queries, qo_own] + qo_blocks,
        2_150_000_000,
    )

    slice_grad = run(
        slice_grad_kernel, shape((128, 1024), F32), [product, grad_memory], 70_000_000, False
    )
    pieces = lax.all_to_all(slice_grad.reshape(4, 32, 1024), "dp", 0, 0, tiled=True)
    gradient = jnp.sum(pieces, axis=0).astype(BF)
    row = jnp.concatenate(share_plane(gradient, False), axis=0)
    whole = share_plane(row, True)

    input_terms = pl.pallas_call(
        input_grad_kernel,
        out_shape=shape((2, 512, 1024), F32),
        in_specs=[SMEM] + [VMEM] * 17,
        out_specs=VMEM,
        scratch_shapes=[pltpu.VMEM((4, 512, 512), BF)],
        compiler_params=pltpu.CompilerParams(vmem_limit_bytes=48 << 20),
        cost_estimate=pl.CostEstimate(
            flops=4_500_000_000, bytes_accessed=20 << 20, transcendentals=0
        ),
    )(where, query_part, keys, values, grad_memory, kv_own, *kv_blocks)
    sent = lax.dynamic_index_in_dim(input_terms, 1 - core, 0, keepdims=False)
    kept = lax.dynamic_index_in_dim(input_terms, core, 0, keepdims=False)
    arrived = lax.ppermute(sent, "tensor", [(0, 1), (1, 0)])
    input_grad = (kept + arrived).astype(BF).reshape(1, 512, 1024)

    state = shape((512, 1024), F32)
    master_new, moment_new, second_new = run(
        adam_kernel,
        [state, state, state],
        [where, key_master, key_moment, key_second] + whole,
        10_000_000,
    )
    return (input_grad, master_new, moment_new, second_new)


def solution(mesh):
    return jax.shard_map(
        local,
        mesh=mesh,
        in_specs=(
            P("dp", "context", None),
            P("dp", "context", None),
            P("dp", "tensor"),
            P("dp", "tensor"),
            P("dp", "tensor"),
            P("dp", "tensor"),
            P("dp", "tensor"),
            P("dp", "tensor"),
        ),
        out_specs=(
            P("dp", "context", "tensor"),
            P("dp", "tensor"),
            P("dp", "tensor"),
            P("dp", "tensor"),
        ),
        check_vma=False,
    )
```
